32 devices in a mesh: seq: 8 (over y, x, core), tp: 4 (over z).
Axes of the slice: x: 2, y: 2, z: 4, core: 2. Of those that a mesh axis runs over, the one named last changes fastest.
Arguments:
- hidden_in: bfloat16 [2048, 2048], P(('seq', 'tp')), may hold values from -6 to 6
- attention_gain: float32 [2048], replicated, may hold values from 0.1 to 1.9
- attention_trainer_copy: float32 [2048, 5120], P(('seq', 'tp')), may hold values from -0.125 to 0.125
- query_gain: float32 [128], replicated, may hold values from 0.1 to 1.9
- key_gain: float32 [128], replicated, may hold values from 0.1 to 1.9
- output_proj: bfloat16 [4096, 2048], P('tp'), may hold values from -0.09375 to 0.09375
- post_gain: float32 [2048], replicated, may hold values from 0.1 to 1.9
- router_weight: bfloat16 [2048, 16], replicated, may hold values from -0.125 to 0.125
- gate_up_master: float32 [16, 2048, 1536], P(None, ('seq', 'tp')), may hold values from -0.125 to 0.125
- down_weight: bfloat16 [16, 768, 2048], P('seq', 'tp'), may hold values from -0.21875 to 0.21875
- routes: int32 [2048, 8], P(('seq', 'tp')), may hold values from 0 to 15, all different within a row; in each aligned block of 64 rows (0 to 63, 64 to 127, ...) at most 64 rows name the same one
- lengths: int32 [8], P('seq'), may hold values from 1 to 256, 1024 in all
- page_table: int32 [8, 2], P('seq'), may hold values from 0 to 3, as said below
Outputs:
- hidden_leaving: bfloat16 [2048, 2048], P(('seq', 'tp'))
- cache_pages: bfloat16 [32, 2, 4, 128, 128], P('seq', None, 'tp')
The draws below stay inside these ranges and needn't reach their ends.
Inputs may be any that keep to these rules, and one draw needn't show every extreme that they name: `routes`: each row names 8 different experts. In each aligned block of 64 rows (the rows of one device) no expert is named by more than 64 rows, a bound that some block reaches. `lengths`: some prompt has exactly 256 live positions. `page_table`: the 2 slots of one prompt are distinct.
All inputs are finite; a program needn't handle non-finite values. No bound on the sum of `lengths` on one device may be relied on, other than what follows from the above.
Results may differ from the reference program's by a relative error of at most 0.0085.
Values may be sent and summed in bfloat16 or wider, within the bound.
A program may use at most 128 MiB of HBM per device.

```python
import math
import jax
import jax.numpy as jnp
import numpy as np
from jax import lax

D = 2048
QUERY_HEADS = 32
KEY_VALUE_HEADS = 4
HEAD_SIZE = 128
FF = 768
TOPK = 8
PAGE_POSITIONS = 128
PADDED_LENGTH = 256
E = 16
QKVW = 5120
CAP = 64
PROMPTS = 8
TOKENS = 2048
PROMPT_PAGES = 2
PROMPT_SLOTS = 4
CACHE_SLOTS = 32
N_SEQ = 8
N_TP = 4


def draw_page_table(key, part):
    keys_all = jax.random.split(jax.random.fold_in(key, 7), PROMPTS)

    def one_prompt(prompt_key):
        return jax.random.permutation(prompt_key, PROMPT_SLOTS)[:PROMPT_PAGES]
    return jax.vmap(one_prompt)(keys_all).astype(jnp.int32)


def shard_levels(key, extent, shards, low, high):
    def one(axis_at, parts):
        steps = jax.random.uniform(jax.random.fold_in(jax.random.fold_in(key, 6), axis_at), (parts,), jnp.float32, low / len(shards), high / len(shards))
        return jnp.repeat(jnp.exp(steps), extent[axis_at] // parts).reshape((-1,) + (1,) * (len(extent) - axis_at - 1))

    level = one(*shards[0])
    for cut in shards[1:]:
        level = level * one(*cut)
    return level


def length_profile(count, total, bound, lean):
    loads = [(1 << 20) // math.isqrt(rank ** lean) + 1 for rank in range(2, count + 1)]
    spare, given = total - bound - (count - 1), [1] * (count - 1)
    while spare > 0:
        free = [i for i in range(count - 1) if given[i] < bound]
        whole, budget = sum([loads[i] for i in free]), spare
        for i in free:
            addition = min(bound - given[i], max(1, budget * loads[i] // whole), spare)
            given[i] = given[i] + addition
            spare = spare - addition
    return np.array([bound] + given)


def uneven(stream_key, count, total, reach, lean):
    if count == 2:
        one = jax.random.randint(stream_key, (), max(1, total - reach), min(reach, total - 1) + 1)
        return jnp.stack([one, total - one])
    sizes = jnp.asarray(length_profile(count, total, reach, lean), jnp.int32)
    couples = (count - 1) // 2
    source_of, receiver = sizes[1:1 + 2 * couples:2], sizes[2:2 + 2 * couples:2]
    room = jnp.minimum(source_of - 1, reach - receiver)
    passed = jax.random.randint(jax.random.fold_in(stream_key, 1), (couples,), 0, 1 << 20) % (room + 1)
    sizes = sizes.at[1:1 + 2 * couples:2].set(source_of - passed).at[2:2 + 2 * couples:2].set(receiver + passed)
    return sizes[jax.random.permutation(jax.random.fold_in(stream_key, 2), count)]


def assign_block(own_key, own, number, rows, count, top, reach, lean):
    order = jax.random.permutation(own_key, count)
    crowded, ordinary = portions_of(count, rows * top, reach, lean, True), portions_of(count, rows * top, reach, lean, False)
    places = jnp.arange(count)

    def named(tallies, turn):
        used = int((tallies > 0).sum())
        fixed = max(1, used // 4)
        shifted = fixed + (places - fixed + turn * (used - fixed)) % max(1, count - fixed)
        return jnp.zeros((count,), jnp.int32).at[order[jnp.where(places < fixed, places, shifted)]].set(jnp.asarray(tallies, jnp.int32))

    tallies = jnp.where(number % 4 == 0, named(crowded, number // 4), named(ordinary, number - number // 4 - 1))
    mixed = jax.random.permutation(jax.random.fold_in(own, 3), count)
    giver, receiver = mixed[0:count // 2 * 2:2], mixed[1:count // 2 * 2:2]
    margin = jnp.minimum(tallies[giver] - 1, reach - tallies[receiver]) // 2
    margin = jnp.where((giver == order[0]) | (receiver == order[0]) | (tallies[receiver] == 0), 0, jnp.maximum(margin, 0))
    shifted = jax.random.randint(jax.random.fold_in(own, 4), (count // 2,), 0, 1 << 20) % (margin + 1)
    tallies = tallies.at[giver].add(-shifted).at[receiver].add(shifted)
    items = jnp.searchsorted(jnp.cumsum(tallies), jnp.arange(rows * top), side="right").astype(jnp.int32)
    listing = items.reshape(top, rows).T
    listing = listing[jax.random.permutation(jax.random.fold_in(own, 1), rows)]
    turn = jax.random.randint(jax.random.fold_in(own, 2), (rows, 1), 0, top)
    return jnp.take_along_axis(listing, (jnp.arange(top)[None, :] + turn) % top, axis=1)


def portions_of(number_of, total, limit, slope, full):
    portions = [(1 << 20) // math.isqrt(grade ** slope) + 1 for grade in range(1, number_of + 1)]
    largest = limit if full else min(limit, max(-(-total // number_of), total * portions[0] // sum(portions)))
    least = 1 if total - largest >= number_of - 1 else 0
    holding, surplus = [largest] + [least] * (number_of - 1), total - largest - least * (number_of - 1)
    while surplus > 0:
        free = [i for i in range(1, number_of) if holding[i] < largest] or [i for i in range(1, number_of) if holding[i] < limit]
        pool, remaining = sum([portions[i] for i in free]), surplus
        for i in free:
            addition = min(limit - holding[i], max(1, remaining * portions[i] // pool), surplus)
            holding[i] = holding[i] + addition
            surplus = surplus - addition
    return np.array(holding)


def scatter_about(rng, dims, width, limit, pieces=(), held_as=jnp.bfloat16):
    drawn = jax.random.normal(rng, dims, jnp.float32) * width
    if len(pieces) > 0:
        drawn = shard_levels(rng, dims, pieces, -0.22, 0.18) * drawn
    return jnp.clip(drawn, min=-limit, max=limit).astype(held_as)


def setup_inputs(seed: int = 0) -> dict:
    key_of = jax.random.split(jax.random.key(seed), 14)
    hidden_in = scatter_about(key_of[0], (TOKENS, D), 1.0, 6.0, ((0, 32),))
    attention_gain = jnp.clip(1.0 + 0.18 * jax.random.normal(key_of[1], (D,), jnp.float32), 0.1, 1.9)
    attention_trainer_copy = scatter_about(key_of[2], (D, QKVW), D ** -0.5, 0.125, ((0, 32),), jnp.float32)
    query_gain = jnp.clip(1.0 + 0.18 * jax.random.normal(key_of[3], (HEAD_SIZE,), jnp.float32), 0.1, 1.9)
    key_gain = jnp.clip(1.0 + 0.18 * jax.random.normal(key_of[4], (HEAD_SIZE,), jnp.float32), 0.1, 1.9)
    output_proj = scatter_about(key_of[5], (QUERY_HEADS * HEAD_SIZE, D), (QUERY_HEADS * HEAD_SIZE) ** -0.5, 0.09375, ((0, 4),))
    post_gain = jnp.clip(1.0 + 0.18 * jax.random.normal(key_of[6], (D,), jnp.float32), 0.1, 1.9)
    router_weight = scatter_about(key_of[7], (D, E), D ** -0.5, 0.125)
    gate_up_master = scatter_about(key_of[8], (E, D, 2 * FF), D ** -0.5, 0.125, ((1, 32),), jnp.float32)
    down_weight = scatter_about(key_of[9], (E, FF, D), FF ** -0.5, 0.21875, ((0, 8), (1, 4)))
    routes_keys = jax.random.split(jax.random.fold_in(key_of[10], 1), TOKENS // (PADDED_LENGTH // N_TP))
    routes_turns = jax.random.permutation(jax.random.fold_in(key_of[10], 3), TOKENS // (PADDED_LENGTH // N_TP))
    routes = jax.vmap(lambda own, number: assign_block(jax.random.fold_in(key_of[10], 2), own, number, PADDED_LENGTH // N_TP, E, TOPK, CAP, 1))(routes_keys, routes_turns).reshape((TOKENS, TOPK))
    lengths = uneven(key_of[11], PROMPTS, PROMPTS * PADDED_LENGTH // 2, PADDED_LENGTH, 2).astype(jnp.int32)
    page_table = draw_page_table(jax.random.fold_in(key_of[13], 71), 0)
    return {"hidden_in": hidden_in, "attention_gain": attention_gain, "attention_trainer_copy": attention_trainer_copy, "query_gain": query_gain, "key_gain": key_gain, "output_proj": output_proj, "post_gain": post_gain, "router_weight": router_weight, "gate_up_master": gate_up_master, "down_weight": down_weight, "routes": routes, "lengths": lengths, "page_table": page_table}


EPS = 1e-06
THETA = 1000000.0

def rms_scale(values, gain):
    return values * lax.rsqrt(lax.optimization_barrier(jnp.mean(values * values, axis=-1, keepdims=True)) + EPS) * gain

def rotate(values, positions):
    half_dim = values.shape[-1] // 2
    frequency = THETA ** (-2.0 * jnp.arange(half_dim, dtype=jnp.float32) / values.shape[-1])
    angles = positions.astype(jnp.float32)[:, None] * frequency[None, :]
    cosine = jnp.cos(angles)[:, None, :]
    sine = jnp.sin(angles)[:, None, :]
    first_half = values[..., :half_dim]
    second_half = values[..., half_dim:]
    return jnp.concatenate([first_half * cosine - second_half * sine, second_half * cosine + first_half * sine], axis=-1)

def attend_prompt(query_rows, keys_rotated, values_in, prompt_length):
    column_span = query_rows.shape[0]
    scores = jnp.einsum('qhgd,khd->hgqk', query_rows.astype(jnp.float32), keys_rotated.astype(jnp.float32)) / math.sqrt(query_rows.shape[-1])
    places = jnp.arange(column_span)
    allowed = (places[None, :] <= places[:, None]) & (places[None, :] < prompt_length)
    weights = jnp.where(allowed, jnp.exp(scores), 0.0)
    probs = (weights / lax.optimization_barrier(jnp.sum(weights, axis=-1, keepdims=True))).astype(jnp.bfloat16)
    context_rows = jnp.einsum('hgqk,khd->qhgd', probs.astype(jnp.float32), values_in.astype(jnp.float32))
    return context_rows.astype(jnp.bfloat16).reshape(column_span, -1)

def reference(hidden_in, attention_gain, attention_trainer_copy, query_gain, key_gain, output_proj, post_gain, router_weight, gate_up_master, down_weight, routes, lengths, page_table):
    query_group_width = QUERY_HEADS // KEY_VALUE_HEADS
    inputs = hidden_in.astype(jnp.float32)
    normed = rms_scale(inputs, attention_gain).astype(jnp.bfloat16)
    attention_weight = lax.optimization_barrier(attention_trainer_copy.astype(jnp.bfloat16))
    projected_rows = jnp.einsum('td,dc->tc', normed.astype(jnp.float32), attention_weight.astype(jnp.float32))
    positions = jnp.arange(PADDED_LENGTH)
    query_all = projected_rows[:, :QUERY_HEADS * HEAD_SIZE].reshape(N_SEQ, PADDED_LENGTH, QUERY_HEADS, HEAD_SIZE)
    key_gathered = projected_rows[:, QUERY_HEADS * HEAD_SIZE:(QUERY_HEADS + KEY_VALUE_HEADS) * HEAD_SIZE].reshape(N_SEQ, PADDED_LENGTH, KEY_VALUE_HEADS, HEAD_SIZE)
    value_gathered = projected_rows[:, (QUERY_HEADS + KEY_VALUE_HEADS) * HEAD_SIZE:].reshape(N_SEQ, PADDED_LENGTH, KEY_VALUE_HEADS, HEAD_SIZE).astype(jnp.bfloat16)
    query_all = jax.vmap(lambda prompt_block: rotate(rms_scale(prompt_block, query_gain), positions))(query_all).astype(jnp.bfloat16)
    key_gathered = jax.vmap(lambda prompt_block: rotate(rms_scale(prompt_block, key_gain), positions))(key_gathered).astype(jnp.bfloat16)

    def one_prompt(items):
        query_local, key_local, value_local, prompt_length = items
        return attend_prompt(query_local.reshape(PADDED_LENGTH, KEY_VALUE_HEADS, query_group_width, HEAD_SIZE), key_local, value_local, prompt_length)
    context_rows = lax.map(one_prompt, (query_all, key_gathered, value_gathered, lengths)).reshape(TOKENS, QUERY_HEADS * HEAD_SIZE)
    after_attn = inputs + jnp.einsum('tc,cd->td', context_rows.astype(jnp.float32), output_proj.astype(jnp.float32))
    mixed = rms_scale(after_attn, post_gain).astype(jnp.bfloat16)
    logits = jnp.einsum('td,de->te', mixed.astype(jnp.float32), router_weight.astype(jnp.float32))
    chosen = jnp.take_along_axis(logits, routes, axis=1)
    raised = jnp.exp(chosen)
    gates = raised / lax.optimization_barrier(jnp.sum(raised, axis=1, keepdims=True))
    pair_count = TOKENS * TOPK
    most_rows = N_SEQ * N_TP * CAP
    quarter_units = FF // N_TP
    flat_expert = routes.reshape(-1).astype(jnp.int32)
    order = jnp.argsort(flat_expert, stable=True).astype(jnp.int32)
    counts = lax.optimization_barrier(jnp.sum((flat_expert[:, None] == jnp.arange(E, dtype=jnp.int32)[None, :]).astype(jnp.int32), axis=0)).astype(jnp.int32)
    starts = (jnp.cumsum(counts) - counts).astype(jnp.int32)
    token_sorted = jnp.concatenate([order // TOPK, jnp.zeros((most_rows,), jnp.int32)]).astype(jnp.int32)

    def one_expert(expert):
        picked = lax.dynamic_slice_in_dim(token_sorted, starts[expert], most_rows)
        expert_rows = mixed[picked]
        weight_here = lax.optimization_barrier(gate_up_master[expert].astype(jnp.bfloat16))
        both = jnp.einsum('md,df->mf', expert_rows.astype(jnp.float32), weight_here.astype(jnp.float32))
        units = (jax.nn.silu(both[:, :FF]) * both[:, FF:]).astype(jnp.bfloat16)
        partial_sums = jnp.einsum('mqf,qfd->qmd', units.reshape(most_rows, N_TP, quarter_units).astype(jnp.float32), down_weight[expert].reshape(N_TP, quarter_units, D).astype(jnp.float32))
        rounded = lax.optimization_barrier(partial_sums.astype(jnp.bfloat16))
        return lax.optimization_barrier(jnp.sum(rounded.astype(jnp.float32), axis=0)).astype(jnp.bfloat16)
    expert_table = lax.map(one_expert, jnp.arange(E, dtype=jnp.int32))
    sorted_expert = flat_expert[order]
    offsets = (jnp.arange(pair_count, dtype=jnp.int32) - starts[sorted_expert]).astype(jnp.int32)
    sorted_out = expert_table[sorted_expert, offsets]
    expert_out = jnp.zeros((pair_count, D), jnp.bfloat16).at[order].set(sorted_out)
    combined = lax.optimization_barrier(jnp.sum(gates[:, :, None] * expert_out.reshape(TOKENS, TOPK, D).astype(jnp.float32), axis=1))
    live_rows = jnp.tile(positions, N_SEQ) < jnp.repeat(lengths, PADDED_LENGTH)
    hidden_leaving = jnp.where(live_rows[:, None], after_attn + combined, 0.0).astype(jnp.bfloat16)
    live = (positions[None, :] < lengths[:, None])[:, :, None, None]
    zero_value = jnp.zeros((), jnp.bfloat16)
    keys_kept = jnp.where(live, key_gathered, zero_value)
    values_kept = jnp.where(live, value_gathered, zero_value)
    prompt_pages = jnp.stack([keys_kept, values_kept], axis=2)
    prompt_pages = prompt_pages.reshape(N_SEQ, PROMPT_PAGES, PAGE_POSITIONS, 2, KEY_VALUE_HEADS, HEAD_SIZE).transpose(0, 1, 3, 4, 2, 5)
    paged_cache = jnp.zeros((N_SEQ, PROMPT_SLOTS, 2, KEY_VALUE_HEADS, PAGE_POSITIONS, HEAD_SIZE), jnp.bfloat16)
    paged_cache = paged_cache.at[jnp.arange(N_SEQ, dtype=jnp.int32)[:, None], page_table].set(prompt_pages)
    return (hidden_leaving, paged_cache.reshape(CACHE_SLOTS, 2, KEY_VALUE_HEADS, PAGE_POSITIONS, HEAD_SIZE))
```

```python
import math

import jax
import jax.numpy as jnp
from jax import lax
from jax.sharding import Mesh, PartitionSpec as P

QUERY_HEADS = 32
KEY_VALUE_HEADS = 4
HEAD_SIZE = 128
FF = 768
TOPK = 8
PAGE_POSITIONS = 128


EPS = 1e-06
THETA = 1000000.0


def rms_scale(values, gain):
    return values * lax.rsqrt(jnp.mean(values * values, axis=-1, keepdims=True) + EPS) * gain


def rotate(values, positions):
    half_dim = values.shape[-1] // 2
    frequency = THETA ** (-2.0 * jnp.arange(half_dim, dtype=jnp.float32) / values.shape[-1])
    angles = positions.astype(jnp.float32)[:, None] * frequency[None, :]
    cosine = jnp.cos(angles)[:, None, :]
    sine = jnp.sin(angles)[:, None, :]
    first_half = values[..., :half_dim]
    second_half = values[..., half_dim:]
    return jnp.concatenate(
        [first_half * cosine - second_half * sine, second_half * cosine + first_half * sine],
        axis=-1,
    )


def attend_prompt(query_rows, keys_rotated, values_in, prompt_length):
    column_span = query_rows.shape[0]
    scores = jnp.einsum(
        "qhgd,khd->hgqk", query_rows, keys_rotated, preferred_element_type=jnp.float32
    ) / math.sqrt(query_rows.shape[-1])
    places = jnp.arange(column_span)
    allowed = (places[None, :] <= places[:, None]) & (places[None, :] < prompt_length)
    weights = jnp.where(allowed, jnp.exp(scores), 0.0)
    probs = (weights / jnp.sum(weights, axis=-1, keepdims=True)).astype(jnp.bfloat16)
    context_rows = jnp.einsum(
        "hgqk,khd->qhgd", probs, values_in, preferred_element_type=jnp.float32
    )
    return context_rows.astype(jnp.bfloat16).reshape(column_span, -1)


def name_experts(routes, experts_all):
    experts = jnp.arange(experts_all, dtype=jnp.int32)
    return jnp.any(routes[:, :, None] == experts[None, None, :], axis=1)


def regroup(features, seq_count, tensor_parallel_count):
    leading = features.shape[:-1]
    blocks = features.reshape(leading + (seq_count, tensor_parallel_count, -1))
    return jnp.swapaxes(blocks, -3, -2).reshape(leading + (-1,))


def on_device_dispatch(
    hidden_in,
    attention_gain,
    attention_trainer_copy,
    query_gain,
    key_gain,
    output_proj,
    post_gain,
    router_weight,
    gate_up_master,
    down_weight,
    routes,
    lengths,
    page_table,
):
    tensor_parallel_count = lax.axis_size("tp")
    seq_count = lax.axis_size("seq")
    tp_place = lax.axis_index("tp")
    quarter = hidden_in.shape[0]
    width = hidden_in.shape[1]
    experts_all = router_weight.shape[1]
    exp_here = experts_all // seq_count
    capacity = max(2, 2 * quarter * TOPK // experts_all)
    quarter_units = FF // tensor_parallel_count
    heads_here = QUERY_HEADS // tensor_parallel_count
    key_value_local = KEY_VALUE_HEADS // tensor_parallel_count
    prompt_rows = lax.all_gather(hidden_in, "tp", axis=0, tiled=True)
    column_span = prompt_rows.shape[0]
    normed = rms_scale(prompt_rows.astype(jnp.float32), attention_gain).astype(jnp.bfloat16)
    trainer_rows = attention_trainer_copy.shape[0]
    query_cols = attention_trainer_copy[:, : QUERY_HEADS * HEAD_SIZE].reshape(
        trainer_rows, tensor_parallel_count, heads_here * HEAD_SIZE
    )
    key_columns = attention_trainer_copy[
        :, QUERY_HEADS * HEAD_SIZE : (QUERY_HEADS + KEY_VALUE_HEADS) * HEAD_SIZE
    ].reshape(trainer_rows, tensor_parallel_count, key_value_local * HEAD_SIZE)
    value_columns = attention_trainer_copy[
        :, (QUERY_HEADS + KEY_VALUE_HEADS) * HEAD_SIZE :
    ].reshape(trainer_rows, tensor_parallel_count, key_value_local * HEAD_SIZE)
    joined = (
        jnp.concatenate([query_cols, key_columns, value_columns], axis=2)
        .reshape(trainer_rows, -1)
        .astype(jnp.bfloat16)
    )
    head_rows = lax.all_to_all(joined, "tp", split_axis=1, concat_axis=0, tiled=True)
    projected_rows = jnp.dot(
        normed,
        lax.all_gather(head_rows, "seq", axis=0, tiled=True),
        preferred_element_type=jnp.float32,
    )
    positions = jnp.arange(column_span)
    query_rows = projected_rows[:, : heads_here * HEAD_SIZE].reshape(
        column_span, heads_here, HEAD_SIZE
    )
    keys_raw = projected_rows[
        :, heads_here * HEAD_SIZE : (heads_here + key_value_local) * HEAD_SIZE
    ].reshape(column_span, key_value_local, HEAD_SIZE)
    values_local_rows = (
        projected_rows[:, (heads_here + key_value_local) * HEAD_SIZE :]
        .reshape(column_span, key_value_local, HEAD_SIZE)
        .astype(jnp.bfloat16)
    )
    query_rows = rotate(rms_scale(query_rows, query_gain), positions).astype(jnp.bfloat16)
    keys_rotated = rotate(rms_scale(keys_raw, key_gain), positions).astype(jnp.bfloat16)
    prompt_length = lengths[0]
    context_rows = attend_prompt(
        query_rows.reshape(column_span, key_value_local, QUERY_HEADS // KEY_VALUE_HEADS, HEAD_SIZE),
        keys_rotated,
        values_local_rows,
        prompt_length,
    )
    attention_sums = lax.psum_scatter(
        jnp.dot(context_rows, output_proj, preferred_element_type=jnp.float32).astype(jnp.bfloat16),
        "tp",
        scatter_dimension=0,
        tiled=True,
    ).astype(jnp.float32)
    after_attn = hidden_in.astype(jnp.float32) + attention_sums
    mixed = rms_scale(after_attn, post_gain).astype(jnp.bfloat16)
    logits = jnp.dot(mixed, router_weight, preferred_element_type=jnp.float32)
    hits = name_experts(routes, experts_all)
    raised = jnp.where(hits, jnp.exp(logits), 0.0)
    gates = raised / jnp.sum(raised, axis=1, keepdims=True)
    row = jnp.arange(quarter)
    earlier = (row[None, :] < row[:, None]).astype(jnp.bfloat16)
    before = jnp.dot(earlier, hits.astype(jnp.bfloat16), preferred_element_type=jnp.float32)
    before = before.astype(jnp.int32)
    slots = jnp.arange(capacity, dtype=jnp.int32)
    placed = hits[:, :, None] & (before[:, :, None] == slots[None, None, :])
    placed_gates = jnp.where(placed, gates[:, :, None], 0.0).reshape(quarter, -1)
    placed = placed.reshape(quarter, -1).astype(jnp.bfloat16)
    mixed_order = regroup(mixed, seq_count, tensor_parallel_count)
    outgoing = jnp.dot(placed.T, mixed_order, preferred_element_type=jnp.float32).astype(
        jnp.bfloat16
    )
    outgoing = outgoing.reshape(seq_count, exp_here, capacity, width)
    incoming = lax.all_to_all(outgoing, "seq", split_axis=0, concat_axis=0, tiled=True)
    by_expert = lax.all_to_all(
        gate_up_master.astype(jnp.bfloat16), "seq", split_axis=0, concat_axis=1, tiled=True
    )
    full_gate_up, full_down = (
        lax.all_gather(by_expert, "tp", axis=1, tiled=True),
        lax.all_gather(down_weight, "tp", axis=1, tiled=True),
    )
    results = []
    for expert_slot in range(exp_here):
        flat_rows = incoming[:, expert_slot].reshape(-1, width)
        both = jnp.dot(flat_rows, full_gate_up[expert_slot], preferred_element_type=jnp.float32)
        units = (jax.nn.silu(both[:, :FF]) * both[:, FF:]).astype(jnp.bfloat16)
        summed = jnp.zeros((flat_rows.shape[0], width), jnp.float32)
        for block_index in range(tensor_parallel_count):
            lower = block_index * quarter_units
            produced = jnp.dot(
                units[:, lower : lower + quarter_units],
                full_down[expert_slot, lower : lower + quarter_units],
                preferred_element_type=jnp.float32,
            )
            summed = summed + lax.optimization_barrier(produced.astype(jnp.bfloat16)).astype(
                jnp.float32
            )
        results.append(summed.astype(jnp.bfloat16).reshape(seq_count, capacity, width))
    expert_result = jnp.stack(results, axis=1)
    returned = lax.all_to_all(expert_result, "seq", split_axis=0, concat_axis=0, tiled=True)
    combined = jnp.dot(
        placed_gates,
        returned.reshape(experts_all * capacity, width).astype(jnp.float32),
        precision=lax.Precision.HIGHEST,
    )
    own_places = tp_place * quarter + jnp.arange(quarter)
    live_rows = own_places < prompt_length
    hidden_leaving = jnp.where(live_rows[:, None], after_attn + combined, 0.0).astype(jnp.bfloat16)
    return (hidden_leaving, fill_cache(keys_rotated, values_local_rows, prompt_length, page_table))


PLANE = ("chip", "core")
EVERY = ("chip", "core", "tp")
ROWS = ("chip", "tp")
DENSE_BYTES = 16 << 20


def project_and_attend(
    hidden_in, attention_gain, attention_trainer_copy, query_gain, key_gain, prompt_length
):
    tensor_parallel_count = lax.axis_size("tp")
    heads_here = QUERY_HEADS // tensor_parallel_count
    key_value_local = KEY_VALUE_HEADS // tensor_parallel_count
    prompt_rows = lax.all_gather(hidden_in, "tp", axis=0, tiled=True)
    column_span = prompt_rows.shape[0]
    normed = rms_scale(prompt_rows.astype(jnp.float32), attention_gain).astype(jnp.bfloat16)
    trainer_rows = attention_trainer_copy.shape[0]
    query_end = QUERY_HEADS * HEAD_SIZE
    key_end = query_end + KEY_VALUE_HEADS * HEAD_SIZE
    rounded = attention_trainer_copy.astype(jnp.bfloat16)
    parts = [
        part.reshape(trainer_rows, tensor_parallel_count, -1)
        for part in (rounded[:, :query_end], rounded[:, query_end:key_end], rounded[:, key_end:])
    ]
    joined = jnp.concatenate(parts, axis=2).reshape(trainer_rows, -1)
    head_rows = lax.all_to_all(joined, "tp", split_axis=1, concat_axis=0, tiled=True)
    projected_rows = jnp.dot(
        normed,
        lax.all_gather(head_rows, PLANE, axis=0, tiled=True),
        preferred_element_type=jnp.float32,
    )
    positions = jnp.arange(column_span)
    query_rows = projected_rows[:, : heads_here * HEAD_SIZE].reshape(
        column_span, heads_here, HEAD_SIZE
    )
    keys_raw = projected_rows[
        :, heads_here * HEAD_SIZE : (heads_here + key_value_local) * HEAD_SIZE
    ].reshape(column_span, key_value_local, HEAD_SIZE)
    values_rows = (
        projected_rows[:, (heads_here + key_value_local) * HEAD_SIZE :]
        .reshape(column_span, key_value_local, HEAD_SIZE)
        .astype(jnp.bfloat16)
    )
    query_rows = rotate(rms_scale(query_rows, query_gain), positions).astype(jnp.bfloat16)
    keys_rotated = rotate(rms_scale(keys_raw, key_gain), positions).astype(jnp.bfloat16)
    context_rows = attend_prompt(
        query_rows.reshape(column_span, key_value_local, QUERY_HEADS // KEY_VALUE_HEADS, HEAD_SIZE),
        keys_rotated,
        values_rows,
        prompt_length,
    )
    return context_rows, keys_rotated, values_rows


def fill_cache(keys_rotated, values_rows, prompt_length, page_table):
    column_span, key_value_local, _ = keys_rotated.shape
    live = (jnp.arange(column_span) < prompt_length)[:, None, None]
    zero_value = jnp.zeros((), jnp.bfloat16)
    keys_kept = jnp.where(live, keys_rotated, zero_value)
    values_kept = jnp.where(live, values_rows, zero_value)
    pages_here = column_span // PAGE_POSITIONS
    prompt_pages = jnp.stack([keys_kept, values_kept], axis=1)
    prompt_pages = prompt_pages.reshape(
        pages_here, PAGE_POSITIONS, 2, key_value_local, HEAD_SIZE
    ).transpose(0, 2, 3, 1, 4)
    slots = jnp.arange(2 * pages_here, dtype=jnp.int32)[:, None, None, None, None]
    paged_cache = jnp.zeros((2 * pages_here,) + prompt_pages.shape[1:], jnp.bfloat16)
    for page in range(pages_here):
        paged_cache = jnp.where(slots == page_table[0, page], prompt_pages[page][None], paged_cache)
    return paged_cache


def on_device(
    hidden_in,
    attention_gain,
    attention_trainer_copy,
    query_gain,
    key_gain,
    output_proj,
    post_gain,
    router_weight,
    gate_up_master,
    down_weight,
    routes,
    lengths,
    page_table,
):
    tensor_parallel_count = lax.axis_size("tp")
    seq_count = lax.axis_size("chip") * lax.axis_size("core")
    tp_place = lax.axis_index("tp")
    chip_place = lax.axis_index("chip")
    quarter, width = hidden_in.shape
    experts_all = router_weight.shape[1]
    exp_here = experts_all // seq_count
    units_here = FF // tensor_parallel_count
    prompt_length = lengths[0]
    master_rows = gate_up_master.shape[1]
    blocks = (
        gate_up_master.astype(jnp.bfloat16)
        .reshape(seq_count, exp_here, master_rows, 2, tensor_parallel_count, units_here)
        .transpose(0, 4, 2, 3, 1, 5)
        .reshape(seq_count * tensor_parallel_count, master_rows, 2 * exp_here * units_here)
    )
    mine = lax.all_to_all(blocks, EVERY, split_axis=0, concat_axis=0, tiled=True)
    mine = mine.reshape(-1, 2 * exp_here * units_here)
    pair_gate_up = lax.all_gather(mine, "core", axis=0)
    pair_down = lax.all_gather(down_weight.reshape(-1, width), "core", axis=0)
    pair_routes = lax.all_gather(routes, ROWS, axis=0, tiled=True)

    context_rows, keys_rotated, values_rows = project_and_attend(
        hidden_in, attention_gain, attention_trainer_copy, query_gain, key_gain, prompt_length
    )
    attention_sums = lax.psum_scatter(
        jnp.dot(context_rows, output_proj, preferred_element_type=jnp.float32).astype(jnp.bfloat16),
        "tp",
        scatter_dimension=0,
        tiled=True,
    ).astype(jnp.float32)
    after_attn = hidden_in.astype(jnp.float32) + attention_sums
    mixed = rms_scale(after_attn, post_gain).astype(jnp.bfloat16)
    group_rows = lax.all_gather(mixed, "tp", axis=0, tiled=False)
    group_rows = lax.all_gather(group_rows, "chip", axis=0, tiled=True).reshape(-1, width)

    logits = jnp.dot(group_rows, router_weight, preferred_element_type=jnp.float32)
    named = name_experts(pair_routes, experts_all)
    raised = jnp.where(named, jnp.exp(logits), 0.0)
    gates = raised / jnp.sum(raised, axis=1, keepdims=True)
    chip_gates = lax.dynamic_slice_in_dim(gates, chip_place * 2 * exp_here, 2 * exp_here, axis=1)
    column_expert = jnp.arange(exp_here * units_here) // units_here
    halves = []
    for core in range(2):
        both = jnp.dot(group_rows, pair_gate_up[core], preferred_element_type=jnp.float32)
        spread = jnp.zeros((group_rows.shape[0], exp_here * units_here), jnp.float32)
        for slot in range(exp_here):
            gate = chip_gates[:, core * exp_here + slot][:, None]
            spread = jnp.where(column_expert[None, :] == slot, gate, spread)
        hidden_units = exp_here * units_here
        units = jax.nn.silu(both[:, :hidden_units]) * both[:, hidden_units:] * spread
        halves.append(units.astype(jnp.bfloat16))
    partial = jnp.dot(
        jnp.concatenate(halves, axis=1),
        pair_down.reshape(-1, width),
        preferred_element_type=jnp.float32,
    ).astype(jnp.bfloat16)
    combined = lax.psum_scatter(partial, "chip", scatter_dimension=0, tiled=True)
    combined = lax.psum_scatter(combined, "tp", scatter_dimension=0, tiled=True)
    own_places = tp_place * quarter + jnp.arange(quarter)
    live_rows = own_places < prompt_length
    hidden_leaving = jnp.where(
        live_rows[:, None], after_attn + combined.astype(jnp.float32), 0.0
    ).astype(jnp.bfloat16)
    return (hidden_leaving, fill_cache(keys_rotated, values_rows, prompt_length, page_table))


def specs(seq):
    rows = P(seq + ("tp",), None)
    return dict(
        in_specs=(
            rows,
            P(),
            rows,
            P(),
            P(),
            P("tp", None),
            P(),
            P(),
            P(None, seq + ("tp",), None),
            P(seq, "tp", None),
            rows,
            P(seq),
            P(seq, None),
        ),
        out_specs=(rows, P(seq, None, "tp", None, None)),
        check_vma=False,
    )


def solution(mesh):
    seq_count, tensor_parallel_count = mesh.shape["seq"], mesh.shape["tp"]
    cores = Mesh(mesh.devices.reshape(seq_count // 2, 2, tensor_parallel_count), EVERY)

    def layer(hidden_in, *others):
        if hidden_in.size * hidden_in.dtype.itemsize <= DENSE_BYTES:
            run = jax.shard_map(on_device, mesh=cores, **specs(PLANE))
        else:
            run = jax.shard_map(on_device_dispatch, mesh=mesh, **specs(("seq",)))
        return run(hidden_in, *others)

    return layer
```

```python
import functools
import math

import jax
import jax.numpy as jnp
from jax import lax
from jax.experimental import pallas as pl
from jax.experimental.pallas import tpu as pltpu
from jax.sharding import Mesh, PartitionSpec as P

QUERY_HEADS = 32
KEY_VALUE_HEADS = 4
HEAD_SIZE = 128
FF = 768
TOPK = 8
PAGE_POSITIONS = 128


EPS = 1e-06
THETA = 1000000.0


def rms_scale(values, gain):
    return values * lax.rsqrt(jnp.mean(values * values, axis=-1, keepdims=True) + EPS) * gain


def rotate(values, positions):
    half_dim = values.shape[-1] // 2
    frequency = THETA ** (-2.0 * jnp.arange(half_dim, dtype=jnp.float32) / values.shape[-1])
    angles = positions.astype(jnp.float32)[:, None] * frequency[None, :]
    cosine = jnp.cos(angles)[:, None, :]
    sine = jnp.sin(angles)[:, None, :]
    first_half = values[..., :half_dim]
    second_half = values[..., half_dim:]
    return jnp.concatenate(
        [first_half * cosine - second_half * sine, second_half * cosine + first_half * sine],
        axis=-1,
    )


def attend_prompt(query_rows, keys_rotated, values_in, prompt_length):
    column_span = query_rows.shape[0]
    scores = jnp.einsum(
        "qhgd,khd->hgqk", query_rows, keys_rotated, preferred_element_type=jnp.float32
    ) / math.sqrt(query_rows.shape[-1])
    places = jnp.arange(column_span)
    allowed = (places[None, :] <= places[:, None]) & (places[None, :] < prompt_length)
    weights = jnp.where(allowed, jnp.exp(scores), 0.0)
    probs = (weights / jnp.sum(weights, axis=-1, keepdims=True)).astype(jnp.bfloat16)
    context_rows = jnp.einsum(
        "hgqk,khd->qhgd", probs, values_in, preferred_element_type=jnp.float32
    )
    return context_rows.astype(jnp.bfloat16).reshape(column_span, -1)


def name_experts(routes, experts_all):
    experts = jnp.arange(experts_all, dtype=jnp.int32)
    return jnp.any(routes[:, :, None] == experts[None, None, :], axis=1)


def regroup(features, seq_count, tensor_parallel_count):
    leading = features.shape[:-1]
    blocks = features.reshape(leading + (seq_count, tensor_parallel_count, -1))
    return jnp.swapaxes(blocks, -3, -2).reshape(leading + (-1,))


def on_device_dispatch(
    hidden_in,
    attention_gain,
    attention_trainer_copy,
    query_gain,
    key_gain,
    output_proj,
    post_gain,
    router_weight,
    gate_up_master,
    down_weight,
    routes,
    lengths,
    page_table,
):
    tensor_parallel_count = lax.axis_size("tp")
    seq_count = lax.axis_size("seq")
    tp_place = lax.axis_index("tp")
    quarter = hidden_in.shape[0]
    width = hidden_in.shape[1]
    experts_all = router_weight.shape[1]
    exp_here = experts_all // seq_count
    capacity = max(2, 2 * quarter * TOPK // experts_all)
    quarter_units = FF // tensor_parallel_count
    heads_here = QUERY_HEADS // tensor_parallel_count
    key_value_local = KEY_VALUE_HEADS // tensor_parallel_count
    prompt_rows = lax.all_gather(hidden_in, "tp", axis=0, tiled=True)
    column_span = prompt_rows.shape[0]
    normed = rms_scale(prompt_rows.astype(jnp.float32), attention_gain).astype(jnp.bfloat16)
    trainer_rows = attention_trainer_copy.shape[0]
    query_cols = attention_trainer_copy[:, : QUERY_HEADS * HEAD_SIZE].reshape(
        trainer_rows, tensor_parallel_count, heads_here * HEAD_SIZE
    )
    key_columns = attention_trainer_copy[
        :, QUERY_HEADS * HEAD_SIZE : (QUERY_HEADS + KEY_VALUE_HEADS) * HEAD_SIZE
    ].reshape(trainer_rows, tensor_parallel_count, key_value_local * HEAD_SIZE)
    value_columns = attention_trainer_copy[
        :, (QUERY_HEADS + KEY_VALUE_HEADS) * HEAD_SIZE :
    ].reshape(trainer_rows, tensor_parallel_count, key_value_local * HEAD_SIZE)
    joined = (
        jnp.concatenate([query_cols, key_columns, value_columns], axis=2)
        .reshape(trainer_rows, -1)
        .astype(jnp.bfloat16)
    )
    head_rows = lax.all_to_all(joined, "tp", split_axis=1, concat_axis=0, tiled=True)
    projected_rows = jnp.dot(
        normed,
        lax.all_gather(head_rows, "seq", axis=0, tiled=True),
        preferred_element_type=jnp.float32,
    )
    positions = jnp.arange(column_span)
    query_rows = projected_rows[:, : heads_here * HEAD_SIZE].reshape(
        column_span, heads_here, HEAD_SIZE
    )
    keys_raw = projected_rows[
        :, heads_here * HEAD_SIZE : (heads_here + key_value_local) * HEAD_SIZE
    ].reshape(column_span, key_value_local, HEAD_SIZE)
    values_local_rows = (
        projected_rows[:, (heads_here + key_value_local) * HEAD_SIZE :]
        .reshape(column_span, key_value_local, HEAD_SIZE)
        .astype(jnp.bfloat16)
    )
    query_rows = rotate(rms_scale(query_rows, query_gain), positions).astype(jnp.bfloat16)
    keys_rotated = rotate(rms_scale(keys_raw, key_gain), positions).astype(jnp.bfloat16)
    prompt_length = lengths[0]
    context_rows = attend_prompt(
        query_rows.reshape(column_span, key_value_local, QUERY_HEADS // KEY_VALUE_HEADS, HEAD_SIZE),
        keys_rotated,
        values_local_rows,
        prompt_length,
    )
    attention_sums = lax.psum_scatter(
        jnp.dot(context_rows, output_proj, preferred_element_type=jnp.float32).astype(jnp.bfloat16),
        "tp",
        scatter_dimension=0,
        tiled=True,
    ).astype(jnp.float32)
    after_attn = hidden_in.astype(jnp.float32) + attention_sums
    mixed = rms_scale(after_attn, post_gain).astype(jnp.bfloat16)
    logits = jnp.dot(mixed, router_weight, preferred_element_type=jnp.float32)
    hits = name_experts(routes, experts_all)
    raised = jnp.where(hits, jnp.exp(logits), 0.0)
    gates = raised / jnp.sum(raised, axis=1, keepdims=True)
    row = jnp.arange(quarter)
    earlier = (row[None, :] < row[:, None]).astype(jnp.bfloat16)
    before = jnp.dot(earlier, hits.astype(jnp.bfloat16), preferred_element_type=jnp.float32)
    before = before.astype(jnp.int32)
    slots = jnp.arange(capacity, dtype=jnp.int32)
    placed = hits[:, :, None] & (before[:, :, None] == slots[None, None, :])
    placed_gates = jnp.where(placed, gates[:, :, None], 0.0).reshape(quarter, -1)
    placed = placed.reshape(quarter, -1).astype(jnp.bfloat16)
    mixed_order = regroup(mixed, seq_count, tensor_parallel_count)
    outgoing = jnp.dot(placed.T, mixed_order, preferred_element_type=jnp.float32).astype(
        jnp.bfloat16
    )
    outgoing = outgoing.reshape(seq_count, exp_here, capacity, width)
    incoming = lax.all_to_all(outgoing, "seq", split_axis=0, concat_axis=0, tiled=True)
    by_expert = lax.all_to_all(
        gate_up_master.astype(jnp.bfloat16), "seq", split_axis=0, concat_axis=1, tiled=True
    )
    full_gate_up, full_down = (
        lax.all_gather(by_expert, "tp", axis=1, tiled=True),
        lax.all_gather(down_weight, "tp", axis=1, tiled=True),
    )
    results = []
    for expert_slot in range(exp_here):
        flat_rows = incoming[:, expert_slot].reshape(-1, width)
        both = jnp.dot(flat_rows, full_gate_up[expert_slot], preferred_element_type=jnp.float32)
        units = (jax.nn.silu(both[:, :FF]) * both[:, FF:]).astype(jnp.bfloat16)
        summed = jnp.zeros((flat_rows.shape[0], width), jnp.float32)
        for block_index in range(tensor_parallel_count):
            lower = block_index * quarter_units
            produced = jnp.dot(
                units[:, lower : lower + quarter_units],
                full_down[expert_slot, lower : lower + quarter_units],
                preferred_element_type=jnp.float32,
            )
            summed = summed + lax.optimization_barrier(produced.astype(jnp.bfloat16)).astype(
                jnp.float32
            )
        results.append(summed.astype(jnp.bfloat16).reshape(seq_count, capacity, width))
    expert_result = jnp.stack(results, axis=1)
    returned = lax.all_to_all(expert_result, "seq", split_axis=0, concat_axis=0, tiled=True)
    combined = jnp.dot(
        placed_gates,
        returned.reshape(experts_all * capacity, width).astype(jnp.float32),
        precision=lax.Precision.HIGHEST,
    )
    own_places = tp_place * quarter + jnp.arange(quarter)
    live_rows = own_places < prompt_length
    hidden_leaving = jnp.where(live_rows[:, None], after_attn + combined, 0.0).astype(jnp.bfloat16)
    return (hidden_leaving, fill_cache(keys_rotated, values_local_rows, prompt_length, page_table))


PLANE = ("chip", "core")
EVERY = ("chip", "core", "tp")
ROWS = ("chip", "tp")
DENSE_BYTES = 16 << 20


def place_of(index, tensor_parallel_count):
    seq_index = index // tensor_parallel_count
    return (seq_index // 2, seq_index % 2, index % tensor_parallel_count)


def weights_kernel(
    chips, tensors, query_width, key_width, rounded, gate_up, down, columns, pair_gate_up,
    pair_down, send, recv, local,
):
    chip, core, tp = lax.axis_index("chip"), lax.axis_index("core"), lax.axis_index("tp")
    seq = chip * 2 + core
    me = seq * tensors + tp
    total = chips * 2 * tensors
    partner = (chip, 1 - core, tp)
    rows = rounded.shape[0]
    prompt = rows * tensors
    exp_here = pair_gate_up.shape[1]
    block = pair_gate_up.shape[3]
    key_start = query_width * tensors
    pieces = (
        (0, query_width, 0),
        (key_start, key_width, query_width),
        (key_start + key_width * tensors, key_width, query_width + key_width),
    )

    def remote(source, target, number, device):
        return pltpu.make_async_remote_copy(
            src_ref=source,
            dst_ref=target,
            send_sem=send.at[number],
            recv_sem=recv.at[number],
            device_id=device,
            device_id_type=pl.DeviceIdType.MESH,
        )

    def wait(reference, semaphore):
        pltpu.make_async_copy(reference, reference, semaphore).wait()

    barrier = pltpu.get_barrier_semaphore()

    @pl.loop(1, total)
    def _(step):
        pl.semaphore_signal(
            barrier,
            inc=1,
            device_id=place_of((me + step) % total, tensors),
            device_id_type=pl.DeviceIdType.MESH,
        )

    pl.semaphore_wait(barrier, total - 1)

    own_rows = pl.ds(pl.multiple_of(me * rows, rows), rows)

    def column_parts(target_tp):
        for start, size, landing in pieces:
            yield (
                rounded.at[:, pl.ds(pl.multiple_of(start + target_tp * size, 128), size)],
                columns.at[own_rows, pl.ds(landing, size)],
            )

    def unit_part(target_seq, target_tp, target_core):
        return (
            gate_up.at[
                pl.ds(target_seq * exp_here, exp_here),
                :,
                pl.ds(pl.multiple_of(target_tp * block, 128), block),
            ],
            pair_gate_up.at[target_core, :, own_rows, :],
        )

    for step in range(1, tensors):
        target_tp = (tp + step) % tensors
        for source, target in column_parts(target_tp):
            remote(source, target, 0, (chip, core, target_tp)).start()
    for source, target in column_parts(tp):
        pltpu.make_async_copy(source, target, local.at[0]).start()
    pltpu.make_async_copy(*unit_part(seq, tp, core), local.at[1]).start()
    pltpu.make_async_copy(down, pair_down.at[core], local.at[2]).start()

    @pl.loop(1, total)
    def _(step):
        place = place_of((me + step) % total, tensors)
        source, target = unit_part(place[0] * 2 + place[1], place[2], place[1])
        remote(source, target, 1, place).start()

    remote(down, pair_down.at[core], 2, partner).start()

    wait(columns.at[pl.ds(0, prompt - rows)], recv.at[0])
    wait(columns.at[pl.ds(0, rows)], local.at[0])

    def prompt_part(chip_index):
        start = pl.multiple_of((chip_index * 2 + core) * prompt, prompt)
        return columns.at[pl.ds(start, prompt)]

    for step in range(1, chips):
        remote(prompt_part(chip), prompt_part(chip), 3, ((chip + step) % chips, core, tp)).start()
    remote(prompt_part(chip), prompt_part(chip), 4, partner).start()
    wait(columns.at[pl.ds(0, (chips - 1) * prompt)], recv.at[3])
    for step in range(1, chips):
        other = (chip + step) % chips
        remote(prompt_part(other), prompt_part(other), 4, partner).start()

    wait(pair_gate_up.at[0, :, pl.ds(0, (total - 1) * rows), :], recv.at[1])
    wait(pair_gate_up.at[0, :, pl.ds(0, rows), :], local.at[1])
    remote(pair_gate_up.at[core], pair_gate_up.at[core], 5, partner).start()

    wait(columns.at[pl.ds(0, chips * prompt)], recv.at[4])
    wait(pair_down.at[0], recv.at[2])
    wait(pair_down.at[0], local.at[2])
    wait(pair_gate_up.at[0], recv.at[5])
    wait(columns.at[pl.ds(0, prompt - rows)], send.at[0])
    wait(pair_gate_up.at[0, :, pl.ds(0, (total - 1) * rows), :], send.at[1])
    wait(pair_down.at[0], send.at[2])
    wait(columns.at[pl.ds(0, (chips - 1) * prompt)], send.at[3])
    wait(columns.at[pl.ds(0, chips * prompt)], send.at[4])
    wait(pair_gate_up.at[0], send.at[5])


def move_weights(rounded, gate_up, down):
    chips, tensors = lax.axis_size("chip"), lax.axis_size("tp")
    rows = rounded.shape[0]
    all_rows = rows * chips * 2 * tensors
    exp_here = gate_up.shape[0] // (chips * 2)
    block = gate_up.shape[2] // tensors
    query_width = QUERY_HEADS * HEAD_SIZE // tensors
    key_width = KEY_VALUE_HEADS * HEAD_SIZE // tensors
    anywhere = pl.BlockSpec(memory_space=pl.ANY)
    return pl.pallas_call(
        functools.partial(weights_kernel, chips, tensors, query_width, key_width),
        out_shape=(
            jax.ShapeDtypeStruct((all_rows, query_width + 2 * key_width), jnp.bfloat16),
            jax.ShapeDtypeStruct((2, exp_here, all_rows, block), jnp.bfloat16),
            jax.ShapeDtypeStruct((2,) + down.shape, jnp.bfloat16),
        ),
        in_specs=[anywhere] * 3,
        out_specs=(anywhere,) * 3,
        scratch_shapes=[
            pltpu.SemaphoreType.DMA((6,)),
            pltpu.SemaphoreType.DMA((6,)),
            pltpu.SemaphoreType.DMA((3,)),
        ],
        compiler_params=pltpu.CompilerParams(collective_id=0, has_side_effects=True),
    )(rounded, gate_up, down)


def project_and_attend(
    hidden_in, attention_gain, attention_columns, query_gain, key_gain, prompt_length
):
    tensor_parallel_count = lax.axis_size("tp")
    heads_here = QUERY_HEADS // tensor_parallel_count
    key_value_local = KEY_VALUE_HEADS // tensor_parallel_count
    prompt_rows = lax.all_gather(hidden_in, "tp", axis=0, tiled=True)
    column_span = prompt_rows.shape[0]
    normed = rms_scale(prompt_rows.astype(jnp.float32), attention_gain).astype(jnp.bfloat16)
    projected_rows = jnp.dot(
        normed,
        attention_columns,
        preferred_element_type=jnp.float32,
    )
    positions = jnp.arange(column_span)
    query_rows = projected_rows[:, : heads_here * HEAD_SIZE].reshape(
        column_span, heads_here, HEAD_SIZE
    )
    keys_raw = projected_rows[
        :, heads_here * HEAD_SIZE : (heads_here + key_value_local) * HEAD_SIZE
    ].reshape(column_span, key_value_local, HEAD_SIZE)
    values_rows = (
        projected_rows[:, (heads_here + key_value_local) * HEAD_SIZE :]
        .reshape(column_span, key_value_local, HEAD_SIZE)
        .astype(jnp.bfloat16)
    )
    query_rows = rotate(rms_scale(query_rows, query_gain), positions).astype(jnp.bfloat16)
    keys_rotated = rotate(rms_scale(keys_raw, key_gain), positions).astype(jnp.bfloat16)
    context_rows = attend_prompt(
        query_rows.reshape(column_span, key_value_local, QUERY_HEADS // KEY_VALUE_HEADS, HEAD_SIZE),
        keys_rotated,
        values_rows,
        prompt_length,
    )
    return context_rows, keys_rotated, values_rows


def fill_cache(keys_rotated, values_rows, prompt_length, page_table):
    column_span, key_value_local, _ = keys_rotated.shape
    live = (jnp.arange(column_span) < prompt_length)[:, None, None]
    zero_value = jnp.zeros((), jnp.bfloat16)
    keys_kept = jnp.where(live, keys_rotated, zero_value)
    values_kept = jnp.where(live, values_rows, zero_value)
    pages_here = column_span // PAGE_POSITIONS
    prompt_pages = jnp.stack([keys_kept, values_kept], axis=1)
    prompt_pages = prompt_pages.reshape(
        pages_here, PAGE_POSITIONS, 2, key_value_local, HEAD_SIZE
    ).transpose(0, 2, 3, 1, 4)
    slots = jnp.arange(2 * pages_here, dtype=jnp.int32)[:, None, None, None, None]
    paged_cache = jnp.zeros((2 * pages_here,) + prompt_pages.shape[1:], jnp.bfloat16)
    for page in range(pages_here):
        paged_cache = jnp.where(slots == page_table[0, page], prompt_pages[page][None], paged_cache)
    return paged_cache


def on_device(
    hidden_in,
    attention_gain,
    attention_trainer_copy,
    query_gain,
    key_gain,
    output_proj,
    post_gain,
    router_weight,
    gate_up_master,
    down_weight,
    routes,
    lengths,
    page_table,
):
    tensor_parallel_count = lax.axis_size("tp")
    seq_count = lax.axis_size("chip") * lax.axis_size("core")
    tp_place = lax.axis_index("tp")
    chip_place = lax.axis_index("chip")
    quarter, width = hidden_in.shape
    experts_all = router_weight.shape[1]
    exp_here = experts_all // seq_count
    units_here = FF // tensor_parallel_count
    prompt_length = lengths[0]
    column = jnp.arange(2 * FF)
    quarter_of, within = column // (2 * units_here), column % (2 * units_here)
    origin = (within // units_here) * FF + quarter_of * units_here + within % units_here
    selector = (column[:, None] == origin[None, :]).astype(jnp.bfloat16)
    ordered = jnp.dot(
        gate_up_master.astype(jnp.bfloat16).reshape(-1, 2 * FF),
        selector,
        preferred_element_type=jnp.float32,
    ).astype(jnp.bfloat16)
    attention_columns, pair_gate_up, pair_down = move_weights(
        attention_trainer_copy.astype(jnp.bfloat16),
        ordered.reshape(gate_up_master.shape),
        down_weight.reshape(-1, width),
    )
    pair_routes = lax.all_gather(routes, ROWS, axis=0, tiled=True)

    context_rows, keys_rotated, values_rows = project_and_attend(
        hidden_in, attention_gain, attention_columns, query_gain, key_gain, prompt_length
    )
    attention_sums = lax.psum_scatter(
        jnp.dot(context_rows, output_proj, preferred_element_type=jnp.float32).astype(jnp.bfloat16),
        "tp",
        scatter_dimension=0,
        tiled=True,
    ).astype(jnp.float32)
    after_attn = hidden_in.astype(jnp.float32) + attention_sums
    mixed = rms_scale(after_attn, post_gain).astype(jnp.bfloat16)
    group_rows = lax.all_gather(mixed, "tp", axis=0, tiled=False)
    group_rows = lax.all_gather(group_rows, "chip", axis=0, tiled=True).reshape(-1, width)

    logits = jnp.dot(group_rows, router_weight, preferred_element_type=jnp.float32)
    named = name_experts(pair_routes, experts_all)
    raised = jnp.where(named, jnp.exp(logits), 0.0)
    gates = raised / jnp.sum(raised, axis=1, keepdims=True)
    chip_gates = lax.dynamic_slice_in_dim(gates, chip_place * 2 * exp_here, 2 * exp_here, axis=1)
    pieces = []
    for core in range(2):
        for slot in range(exp_here):
            weights = pair_gate_up[core, slot]
            both = jnp.dot(group_rows, weights, preferred_element_type=jnp.float32)
            units = jax.nn.silu(both[:, :units_here]) * both[:, units_here:]
            gate = chip_gates[:, core * exp_here + slot][:, None]
            pieces.append((units * gate).astype(jnp.bfloat16))
    partial = jnp.dot(
        jnp.concatenate(pieces, axis=1),
        pair_down.reshape(-1, width),
        preferred_element_type=jnp.float32,
    ).astype(jnp.bfloat16)
    combined = lax.psum_scatter(partial, "chip", scatter_dimension=0, tiled=True)
    combined = lax.psum_scatter(combined, "tp", scatter_dimension=0, tiled=True)
    own_places = tp_place * quarter + jnp.arange(quarter)
    live_rows = own_places < prompt_length
    hidden_leaving = jnp.where(
        live_rows[:, None], after_attn + combined.astype(jnp.float32), 0.0
    ).astype(jnp.bfloat16)
    return (hidden_leaving, fill_cache(keys_rotated, values_rows, prompt_length, page_table))


def specs(seq):
    rows = P(seq + ("tp",), None)
    return dict(
        in_specs=(
            rows,
            P(),
            rows,
            P(),
            P(),
            P("tp", None),
            P(),
            P(),
            P(None, seq + ("tp",), None),
            P(seq, "tp", None),
            rows,
            P(seq),
            P(seq, None),
        ),
        out_specs=(rows, P(seq, None, "tp", None, None)),
        check_vma=False,
    )


def solution(mesh):
    seq_count, tensor_parallel_count = mesh.shape["seq"], mesh.shape["tp"]
    cores = Mesh(mesh.devices.reshape(seq_count // 2, 2, tensor_parallel_count), EVERY)

    def layer(hidden_in, *others):
        if hidden_in.size * hidden_in.dtype.itemsize <= DENSE_BYTES:
            run = jax.shard_map(on_device, mesh=cores, **specs(PLANE))
        else:
            run = jax.shard_map(on_device_dispatch, mesh=mesh, **specs(("seq",)))
        return run(hidden_in, *others)

    return layer
```
